32 devices in a mesh: group: 2 (over y), request: 4 (over z), tensor: 4 (over x, core).
Axes of the slice: x: 2, y: 2, z: 4, core: 2. Of those that a mesh axis runs over, the one named last changes fastest.
Arguments:
- queries: bfloat16 [8, 384, 8192], P(('group', 'request'), 'tensor'), parts along dimension 0, may hold values from -30 to 30
- kv_new: bfloat16 [8, 384, 2048], P(('group', 'request'), 'tensor'), parts along dimension 0, may hold values from -8 to 8
- pool: bfloat16 [8, 4, 128, 2048], P(('group', 'request'), None, None, 'tensor'), parts along dimension 0, may hold values from -16 to 16
- counts: int32 [8], P('group'), parts along dimension 0, may hold values from 1 to 4, 8 in all
- holder_map: int32 [8, 4], P('group'), parts along dimension 0, may hold values from 0 to 3, each once within a row
Outputs:
- attended: bfloat16 [8, 384, 8192], P(('group', 'request'), 'tensor'), parts along dimension 0
The draws below stay inside these ranges and needn't reach their ends.
There are 2 independent parts, one for each index of `group`. The reference program is written for one: setup_inputs(seed, part) draws one part's arguments, and reference() takes and returns one part's arrays. A program takes and returns all parts, laid end to end along the dimension named above; each array names one. Nothing has to cross between parts.
Inputs may be any that keep to these rules, and one draw needn't show every extreme that they name: Stored span counts; some request has exactly 4. `holder_map`: each row names every rank once.
All inputs are finite; a program needn't handle non-finite values.
Results may differ from the reference program's by a relative error of at most 0.003.
Values may be sent and summed in bfloat16 or wider, within the bound.
No kernel may reach another device: no remote copies, remote signals or barrier semaphores. Data moves between devices by JAX's collectives and lax.ppermute only.
A program may use at most 64 MiB of HBM per device.

```python
import math
import jax
import jax.numpy as jnp
import numpy as np
from jax import lax

HD = 128
QH = 64
KVH = 8
NEW = 384
CH = 128
REQUESTS = 4


def draw_queries(key, part):
    key = jax.random.fold_in(key, 11)
    shape = (REQUESTS, NEW, QH, HD)
    base = jax.random.normal(key, shape, jnp.float32)
    return jnp.clip(base, -30.0, 30.0).reshape(REQUESTS, NEW, QH * HD).astype(jnp.bfloat16)


def draw_pool(key, part):
    key = jax.random.fold_in(key, 23)
    shape = (REQUESTS, REQUESTS, CH, KVH, 2, HD)
    which = jnp.arange(2)[None, None, None, None, :, None]
    factor = jnp.where(which == 0, 3.0, 1.0).astype(jnp.float32)
    base = jax.random.normal(key, shape, jnp.float32) * factor
    return jnp.clip(base, -16.0, 16.0).reshape(REQUESTS, REQUESTS, CH, KVH * 2 * HD).astype(jnp.bfloat16)


def shard_levels(stream_key, extent, pieces, least, high):
    def one(axis_at, blocks):
        steps = jax.random.uniform(jax.random.fold_in(jax.random.fold_in(stream_key, 6), axis_at), (blocks,), jnp.float32, least / len(pieces), high / len(pieces))
        return jnp.repeat(jnp.exp(steps), extent[axis_at] // blocks).reshape((-1,) + (1,) * (len(extent) - axis_at - 1))

    factor_of = one(*pieces[0])
    for cut in pieces[1:]:
        factor_of = factor_of * one(*cut)
    return factor_of


def profile(count, total, reach, slope):
    weights = [(1 << 20) // math.isqrt(rank ** slope) + 1 for rank in range(2, count + 1)]
    rest, given = total - reach - (count - 1), [1] * (count - 1)
    while rest > 0:
        candidates = [i for i in range(count - 1) if given[i] < reach]
        mass, budget = sum([weights[i] for i in candidates]), rest
        for i in candidates:
            addition = min(reach - given[i], max(1, budget * weights[i] // mass), rest)
            given[i] = given[i] + addition
            rest = rest - addition
    return np.array([reach] + given)


def ragged_sizes(stream_key, amount, total, limit, slope):
    if amount == 2:
        one = jax.random.randint(stream_key, (), max(1, total - limit), min(limit, total - 1) + 1)
        return jnp.stack([one, total - one])
    tallies = jnp.asarray(profile(amount, total, limit, slope), jnp.int32)
    pairs = (amount - 1) // 2
    source_of, receiver = tallies[1:1 + 2 * pairs:2], tallies[2:2 + 2 * pairs:2]
    room = jnp.minimum(source_of - 1, limit - receiver)
    passed = jax.random.randint(jax.random.fold_in(stream_key, 1), (pairs,), 0, 1 << 20) % (room + 1)
    tallies = tallies.at[1:1 + 2 * pairs:2].set(source_of - passed).at[2:2 + 2 * pairs:2].set(receiver + passed)
    return tallies[jax.random.permutation(jax.random.fold_in(stream_key, 2), amount)]


def bell_draw(own_key, extent, width, reach, split=(), kind=jnp.bfloat16):
    values = width * jax.random.normal(own_key, extent, jnp.float32)
    if split:
        values = values * shard_levels(own_key, extent, split, -0.22, 0.18)
    return jnp.clip(values, -reach, reach).astype(kind)


def setup_inputs(seed: int = 0, part: int = 0) -> dict:
    key_list = jax.random.split(jax.random.key(seed), 6)
    part_splits = jax.random.split(jax.random.fold_in(key_list[5], part), 6)
    queries = draw_queries(jax.random.fold_in(jax.random.fold_in(key_list[5], part), 71), part)
    kv_new = bell_draw(part_splits[1], (REQUESTS, NEW, KVH * 2 * HD), 1.5, 8.0, ((0, 4), (1, 4)))
    pool = draw_pool(jax.random.fold_in(jax.random.fold_in(key_list[5], part), 71), part)
    counts = ragged_sizes(part_splits[3], REQUESTS, REQUESTS * REQUESTS // 2, REQUESTS, 2).astype(jnp.int32)
    holder_map = jax.vmap(lambda own: jax.random.permutation(own, REQUESTS))(jax.random.split(part_splits[4], REQUESTS)).reshape((REQUESTS, REQUESTS)).astype(jnp.int32)
    return dict(queries=queries, kv_new=kv_new, pool=pool, counts=counts, holder_map=holder_map)


def attend(query, keys_st, values_st, live, keys_own, values_own):
    scale = query.shape[-1] ** -0.5
    s_st = jnp.dot(query, keys_st.T, preferred_element_type=jnp.float32) * scale
    s_own = jnp.dot(query, keys_own.T, preferred_element_type=jnp.float32) * scale
    rows = lax.broadcasted_iota(jnp.int32, s_own.shape, 0)
    cols = lax.broadcasted_iota(jnp.int32, s_own.shape, 1)
    causal = rows >= cols
    s_st = jnp.where(live[None, :], s_st, -jnp.inf)
    s_own = jnp.where(causal, s_own, -jnp.inf)
    peak = jnp.maximum(jnp.max(s_st, axis=1), jnp.max(s_own, axis=1))[:, None]
    p_st = jnp.where(live[None, :], jnp.exp(s_st - peak), 0.0)
    p_own = jnp.where(causal, jnp.exp(s_own - peak), 0.0)
    total = jnp.sum(p_st, axis=1) + jnp.sum(p_own, axis=1)
    acc = jnp.dot(p_st.astype(jnp.bfloat16), values_st, preferred_element_type=jnp.float32)
    acc = acc + jnp.dot(p_own.astype(jnp.bfloat16), values_own, preferred_element_type=jnp.float32)
    return (acc / total[:, None]).astype(jnp.bfloat16)


def reference(queries, kv_new, pool, counts, holder_map):
    group_size = QH // KVH

    def one_request(index):
        q_req = lax.dynamic_index_in_dim(queries, index, 0, keepdims=False)
        q_req = q_req.reshape(NEW, QH, HD).transpose(1, 0, 2)
        own = lax.dynamic_index_in_dim(kv_new, index, 0, keepdims=False).reshape(NEW, KVH, 2, HD)
        stored = lax.dynamic_index_in_dim(pool, index, 1, keepdims=False).reshape(REQUESTS * CH, KVH, 2, HD)
        row = lax.dynamic_index_in_dim(holder_map, index, 0, keepdims=False)
        count = lax.dynamic_index_in_dim(counts, index, 0, keepdims=False)
        ranks = jnp.arange(REQUESTS, dtype=jnp.int32)
        hits = (row[:, None] == ranks[None, :]) & (ranks[:, None] < count)
        valid = jnp.sum(hits.astype(jnp.int32), axis=0) > 0
        live = jnp.repeat(valid, CH)

        def one_head(head):
            kv_head = head // group_size
            query = lax.dynamic_index_in_dim(q_req, head, 0, keepdims=False)
            st = lax.dynamic_index_in_dim(stored, kv_head, 1, keepdims=False)
            ow = lax.dynamic_index_in_dim(own, kv_head, 1, keepdims=False)
            return attend(query, st[:, 0], st[:, 1], live, ow[:, 0], ow[:, 1])

        heads_out = lax.map(one_head, jnp.arange(QH, dtype=jnp.int32))
        return heads_out.transpose(1, 0, 2).reshape(NEW, QH * HD)

    return lax.map(one_request, jnp.arange(REQUESTS, dtype=jnp.int32))
```

```python
import functools
import math

import jax
import jax.numpy as jnp
from jax import lax
from jax.experimental import pallas as pl
from jax.experimental.pallas import tpu as pltpu
from jax.sharding import PartitionSpec as P

HD = 128
NEG = -math.inf
TO_EXP2 = HD**-0.5 * math.log2(math.e)


def hop(piece, size, distance, bit, causal):
    pairs = [
        (i, i ^ bit) for i in range(size) if not causal or (i ^ distance) < (i ^ bit)
    ]
    return lax.ppermute(piece, "tensor", pairs)


def gather_by_distance(piece, size, causal=False):
    held = {0: piece}
    bit = size // 2
    while bit:
        for distance in sorted(held):
            held[distance + bit] = hop(held[distance], size, distance, bit, causal)
        bit //= 2
    return [held[d] for d in range(size)]


def attend_kernel(size, groups, heads, meta, *refs):
    q_ref, new, stored, o_ref = refs[0], refs[1 : 1 + size], refs[1 + size : -1], refs[-1]
    parts = [stored[d * groups : (d + 1) * groups] for d in range(size)]
    me = meta[0]
    tokens = q_ref.shape[0]
    span = stored[0].shape[1]
    spans = sum(part.shape[0] for part in parts[0])
    local_kv = new[0].shape[1] // (2 * HD) // size
    fresh = size * tokens
    keys = fresh + spans * span

    column = lax.broadcasted_iota(jnp.int32, (1, keys), 1)
    bias = jnp.zeros((1, keys), jnp.float32)
    for d in range(1, size):
        hidden = jnp.bitwise_xor(me, d) > me
        here = (column >= tokens * d) & (column < tokens * (d + 1))
        bias = jnp.where(here & hidden, NEG, bias)
    for s in range(spans):
        here = (column >= fresh + s * span) & (column < fresh + (s + 1) * span)
        bias = jnp.where(here & (meta[1 + s] == 0), NEG, bias)
    lead = -(-tokens // HD) * HD
    rows = lax.broadcasted_iota(jnp.int32, (tokens, lead), 0)
    cols = lax.broadcasted_iota(jnp.int32, (tokens, lead), 1)
    lead_bias = jnp.where((rows < cols) & (cols < tokens), NEG, bias[:, :lead])
    ones = jnp.ones((keys, HD), jnp.bfloat16)

    def columns(at, width=HD):
        return pl.ds(pl.multiple_of(at, HD), width)

    def side(d, i, which):
        head = jnp.bitwise_xor(me, d) * local_kv + i
        blocks = [ref[:, columns((2 * head + which) * HD)] for ref in new]
        at = (2 * i + which) * HD
        blocks += [
            part[s, :, at : at + HD] for part in parts[d] for s in range(part.shape[0])
        ]
        return jnp.concatenate(blocks, axis=0)

    def query_columns(d, i, h):
        head = jnp.bitwise_xor(me, d) * local_kv + i
        return columns((head * heads + h) * HD)

    def scores_of(d, i):
        query = jnp.concatenate([q_ref[:, query_columns(d, i, h)] for h in range(heads)], axis=0)
        return lax.dot_general(
            query, side(d, i, 0), (((1,), (1,)), ((), ())), preferred_element_type=jnp.float32
        )

    def finish(d, i, scores):
        value = jnp.concatenate([side(d, i, 1), ones], axis=1)
        scores = scores.reshape(heads, tokens, keys)
        scores = jnp.concatenate(
            [scores[:, :, :lead] + lead_bias[None], scores[:, :, lead:] + bias[:, lead:][None]],
            axis=2,
        ).reshape(heads * tokens, keys)
        peak = jnp.max(scores, axis=1, keepdims=True)
        weights = jnp.exp2((scores - peak) * TO_EXP2).astype(jnp.bfloat16)
        sums = jnp.dot(weights, value, preferred_element_type=jnp.float32)
        out = (sums[:, :HD] / sums[:, HD:]).astype(jnp.bfloat16)
        for h in range(heads):
            o_ref[:, query_columns(d, i, h)] = out[h * tokens : (h + 1) * tokens]

    order = [(d, i) for d in range(size) for i in range(local_kv)]
    scores = scores_of(*order[0])
    for n, at in enumerate(order):
        later = scores_of(*order[n + 1]) if n + 1 < len(order) else None
        finish(*at, scores)
        scores = later


def attend(meta, query, new, stored):
    size = len(new)
    groups = len(stored[0])
    heads = query.shape[1] // new[0].shape[1] * 2
    whole = pl.BlockSpec(memory_space=pltpu.VMEM)
    operands = [query, *new, *(part for parts in stored for part in parts)]
    return pl.pallas_call(
        functools.partial(attend_kernel, size, groups, heads),
        out_shape=jax.ShapeDtypeStruct(query.shape, query.dtype),
        in_specs=[pl.BlockSpec(memory_space=pltpu.SMEM)] + [whole] * len(operands),
        out_specs=whole,
        compiler_params=pltpu.CompilerParams(vmem_limit_bytes=60 * 2**20),
    )(meta, *operands)


def local(size, holders, queries, kv_new, pool, counts, holder_map):
    me = lax.axis_index("request")
    query, new, pool = queries[0], kv_new[0], pool[0]

    def span_of(r):
        return lax.dynamic_index_in_dim(pool, r % holders, 0, keepdims=True)

    own = span_of(me)
    arrived = jnp.concatenate(
        [
            lax.ppermute(span_of(me + s), "request", [(i, (i + s) % holders) for i in range(holders)])
            for s in range(1, holders)
        ],
        axis=0,
    )

    count = lax.dynamic_index_in_dim(counts, me, 0, keepdims=False)
    row = lax.dynamic_index_in_dim(holder_map, me, 0, keepdims=False)
    ranks = jnp.arange(holders, dtype=jnp.int32)
    holder = (me - ranks) % holders
    live = jnp.any((row[:, None] == holder[None, :]) & (ranks[:, None] < count), axis=0)
    meta = jnp.concatenate([lax.axis_index("tensor")[None], live.astype(jnp.int32)])

    new = gather_by_distance(new, size, causal=True)
    near = gather_by_distance(own, size)
    far = gather_by_distance(arrived, size)
    return attend(meta, query, new, list(zip(near, far)))[None]


def solution(mesh):
    placed = (
        P(("group", "request"), "tensor", None),
        P(("group", "request"), "tensor", None),
        P(("group", "request"), None, None, "tensor"),
        P("group"),
        P("group", None),
    )
    return jax.shard_map(
        functools.partial(local, mesh.shape["tensor"], mesh.shape["request"]),
        mesh=mesh,
        in_specs=placed,
        out_specs=P(("group", "request"), "tensor", None),
        check_vma=False,
    )
```

```python
import functools
import math
import typing

import jax
import jax.numpy as jnp
from jax import lax
from jax.experimental import pallas as pl
from jax.experimental.pallas import tpu as pltpu
from jax.sharding import PartitionSpec as P

HD = 128
NEG = -math.inf
CHUNK = 96 * 256
TO_EXP2 = HD**-0.5 * math.log2(math.e)
VMEM = pl.BlockSpec(memory_space=pltpu.VMEM)
SMEM = pl.BlockSpec(memory_space=pltpu.SMEM)
HBM = pl.BlockSpec(memory_space=pltpu.HBM)


def attend_kernel(size, jobs, pieces, states, counts, holder_map, *refs):
    resumed, chained, left, ended = states
    refs = list(refs)

    def take(n):
        return [refs.pop(0) for _ in range(n)]

    (q_ref,) = take(1)
    new = take(size if any(job.fresh for job in jobs) else 0)
    far = dict(zip(pieces, take(len(pieces))))
    peak_in, sums_in = take(2) if resumed else (None, None)
    take(chained)
    peak_out, sums_out = take(2) if left else (None, None)
    o_ref, done, sem = take(3) if ended else (None, None, None)

    me, request = lax.axis_index("tensor"), lax.axis_index("request")
    holders = holder_map.shape[1]
    tokens = q_ref.shape[0]
    local_kv = max(job.head for job in jobs) + 1
    heads = q_ref.shape[1] // HD // (size * local_kv)
    rows = heads * tokens

    def bias_of(job):
        fresh = size * tokens if job.fresh else 0
        sizes = [(first, *far[first, job.distance].shape[:2]) for first in job.far]
        keys = fresh + sum(count * span for _, count, span in sizes)
        column = lax.broadcasted_iota(jnp.int32, (1, keys), 1)
        bias = jnp.zeros((1, keys), jnp.float32)
        if job.fresh:
            for d in range(1, size):
                hidden = jnp.bitwise_xor(me, d) > me
                here = (column >= tokens * d) & (column < tokens * (d + 1))
                bias = jnp.where(here & hidden, NEG, bias)
        start = fresh
        for first, count, span in sizes:
            for c in range(holders):
                place = lax.rem(request - holder_map[request, c] + holders, holders) - first
                at = start + place * span
                here = (column >= at) & (column < at + span)
                here &= (place >= 0) & (place < count) & (c >= counts[request])
                bias = jnp.where(here, NEG, bias)
            start += count * span
        return bias

    lead = -(-tokens // HD) * HD

    def with_causal(bias):
        row = lax.broadcasted_iota(jnp.int32, (tokens, lead), 0)
        col = lax.broadcasted_iota(jnp.int32, (tokens, lead), 1)
        return jnp.where((row < col) & (col < tokens), NEG, bias[:, :lead])

    def kind(job):
        return job.fresh, *((first, far[first, job.distance].shape[0]) for first in job.far)

    biases = {}
    for job in jobs:
        if kind(job) not in biases:
            bias = bias_of(job)
            biases[kind(job)] = bias, with_causal(bias) if job.fresh else None

    def side(job, which):
        blocks = []
        if job.fresh:
            head = jnp.bitwise_xor(me, job.distance) * local_kv + job.head
            at = pl.ds(pl.multiple_of((2 * head + which) * HD, HD), HD)
            blocks += [ref[:, at] for ref in new]
        at = slice((2 * job.head + which) * HD, (2 * job.head + which + 1) * HD)
        for first in job.far:
            piece = far[first, job.distance]
            blocks += [piece[s, :, at] for s in range(piece.shape[0])]
        return jnp.concatenate(blocks, axis=0)

    def columns(job, h=0, count=1):
        head = (jnp.bitwise_xor(me, job.distance) * local_kv + job.head) * heads + h
        return pl.ds(pl.multiple_of(head * HD, HD), count * HD)

    def scores_of(job):
        query = jnp.concatenate([q_ref[:, columns(job, h)] for h in range(heads)], axis=0)
        return lax.dot_general(
            query, side(job, 0), (((1,), (1,)), ((), ())), preferred_element_type=jnp.float32
        )

    copies = []

    def finish(job, scores):
        bias, causal = biases[kind(job)]
        keys = bias.shape[1]
        fit = [n for n in range(16, tokens + 1, 16) if tokens % n == 0 and n * keys <= CHUNK]
        chunk = max(fit, default=16)
        weights, scales = [], []
        for at in range(0, rows, chunk):
            here = slice(at, at + chunk)
            part = scores[here]
            if job.fresh:
                row = at % tokens
                part = jnp.concatenate(
                    [part[:, :lead] + causal[row : row + chunk], part[:, lead:] + bias[:, lead:]],
                    axis=1,
                )
            else:
                part = part + bias
            peak = jnp.broadcast_to(jnp.max(part, axis=1, keepdims=True), (chunk, HD))
            if job.resume is not None:
                before = peak_in[job.resume, here]
                peak = jnp.maximum(peak, before)
                scales.append(jnp.exp2((before - peak) * TO_EXP2))
            if job.leave is not None:
                peak_out[job.leave, here] = peak
            part = part - jnp.concatenate([peak] * (keys // HD), axis=1)
            weights.append(jnp.exp2(part * TO_EXP2).astype(jnp.bfloat16))
        value = side(job, 1)
        value = jnp.concatenate([value, jnp.ones_like(value)], axis=1)
        all_sums = jnp.dot(
            jnp.concatenate(weights, axis=0), value, preferred_element_type=jnp.float32
        )
        slot = len(copies)
        for n, at in enumerate(range(0, rows, chunk)):
            here = slice(at, at + chunk)
            sums = all_sums[here]
            if job.resume is not None:
                sums = sums + sums_in[job.resume, here] * jnp.concatenate([scales[n]] * 2, axis=1)
            if job.leave is not None:
                sums_out[job.leave, here] = sums
            else:
                h, row = at // tokens * HD, at % tokens
                out = (sums[:, :HD] / sums[:, HD:]).astype(o_ref.dtype)
                done[slot, row : row + chunk, h : h + HD] = out
        if job.leave is None:
            copy = pltpu.make_async_copy(
                done.at[slot], o_ref.at[:, columns(job, 0, heads)], sem.at[slot]
            )
            copy.start()
            copies.append(copy)

    scores = scores_of(jobs[0])
    for n, job in enumerate(jobs):
        later = scores_of(jobs[n + 1]) if n + 1 < len(jobs) else None
        finish(job, scores)
        scores = later
    for copy in copies:
        copy.wait()


class Job(typing.NamedTuple):
    distance: int
    head: int
    fresh: bool
    far: tuple
    resume: int | None
    leave: int | None


def attend(rules, query, new, far, jobs, state=None, out=None):
    pieces = tuple(far)
    tokens, columns = query.shape
    _, span, width = far[pieces[0]].shape if far else (0, 0, new[0].shape[1] // len(new))
    local_kv = width // (2 * HD)
    size = new[0].shape[1] // width
    heads = columns // HD // (size * local_kv)
    rows = heads * tokens
    left = sum(job.leave is not None for job in jobs)
    ended = len(jobs) - left
    fresh = any(job.fresh for job in jobs)
    operands = [query, *(new if fresh else ()), *far.values(), *(state or ())]
    chained = [out] if out is not None else []
    keys = [
        size * tokens * job.fresh + sum(far[first, job.distance].shape[0] * span for first in job.far)
        for job in jobs
    ]
    shapes, specs, scratch = [], [], []
    if left:
        shapes += [
            jax.ShapeDtypeStruct((left, rows, HD), jnp.float32),
            jax.ShapeDtypeStruct((left, rows, 2 * HD), jnp.float32),
        ]
        specs += [VMEM, VMEM]
    if ended:
        shapes += [jax.ShapeDtypeStruct(query.shape, query.dtype)]
        specs += [HBM]
        scratch = [
            pltpu.VMEM((ended, tokens, heads * HD), query.dtype),
            pltpu.SemaphoreType.DMA((ended,)),
        ]
    states = (state is not None, len(chained), left, ended)
    results = pl.pallas_call(
        functools.partial(attend_kernel, size, jobs, pieces, states),
        out_shape=shapes,
        in_specs=[SMEM, SMEM] + [VMEM] * len(operands) + [HBM] * len(chained),
        out_specs=specs,
        scratch_shapes=scratch,
        input_output_aliases={2 + len(operands): len(shapes) - 1} if chained else {},
        cost_estimate=pl.CostEstimate(
            flops=8 * HD * rows * sum(keys), bytes_accessed=0, transcendentals=rows * sum(keys)
        ),
        compiler_params=pltpu.CompilerParams(
            vmem_limit_bytes=16 * rows * max(keys) + 10 * 2**20
        ),
    )(*rules, *operands, *chained)
    return (results[:2] if left else None), (results[-1] if ended else None)


def local(size, holders, queries, kv_new, pool, counts, holder_map):
    query, new, pool = queries[0], kv_new[0], pool[0]
    request = lax.axis_index("request")
    rules = (counts, holder_map)
    half = size // 2
    inner = [half >> (n + 1) for n in range(half.bit_length() - 1)]

    def swap(piece, bit):
        return lax.ppermute(piece, "tensor", [(i, i ^ bit) for i in range(size)])

    def spread(piece, bits):
        held = {0: piece}
        for bit in bits:
            for distance in sorted(held):
                held[distance + bit] = swap(held[distance], bit)
        return [held[d] for d in sorted(held)]

    def after(piece, others):
        return lax.optimization_barrier((piece, others))[0]

    def span_of(r):
        return lax.dynamic_index_in_dim(pool, lax.rem(r, holders), 0, keepdims=True)

    new_away = swap(new, half)
    spans = [span_of(request)]
    for s in range(1, holders):
        pairs = [(i, (i + s) % holders) for i in range(holders)]
        spans.append(lax.ppermute(span_of(request + s), "request", pairs))
    early = jnp.concatenate(spans[:2], axis=0)
    early_away = swap(early, half)

    new = spread(new, inner) + spread(new_away, inner)
    local_kv = pool.shape[2] // (2 * HD)
    order = [(d, i) for d in range(size) for i in range(local_kv)]
    home, away = order[: len(order) // 2], order[len(order) // 2 :]

    late_away = swap(jnp.concatenate(spans[2:], axis=0), half)

    far = {(0, d): piece for d, piece in enumerate(spread(jnp.concatenate(spans, axis=0), inner))}
    far |= {(0, half + d): piece for d, piece in enumerate(spread(early_away, inner))}
    jobs = [Job(d, i, True, (0,), None, None) for d, i in home]
    jobs += [Job(d, i, True, (0,), None, n) for n, (d, i) in enumerate(away)]
    state, out = attend(rules, query, new, far, jobs)

    late_away = after(late_away, state)
    far = {(2, half + d): piece for d, piece in enumerate(spread(late_away, inner))}
    jobs = [Job(d, i, False, (2,), n, None) for n, (d, i) in enumerate(away)]
    return attend(rules, query, new, far, jobs, state, out)[1][None]


def solution(mesh):
    placed = (
        P(("group", "request"), "tensor", None),
        P(("group", "request"), "tensor", None),
        P(("group", "request"), None, None, "tensor"),
        P("group"),
        P("group", None),
    )
    return jax.shard_map(
        functools.partial(local, mesh.shape["tensor"], mesh.shape["request"]),
        mesh=mesh,
        in_specs=placed,
        out_specs=P(("group", "request"), "tensor", None),
        check_vma=False,
    )
```

```python
import functools
import math
import typing

import jax
import jax.numpy as jnp
from jax import lax
from jax.experimental import pallas as pl
from jax.experimental.pallas import tpu as pltpu
from jax.sharding import PartitionSpec as P

HD = 128
NEG = -math.inf
CHUNK = 96 * 256
TO_EXP2 = HD**-0.5 * math.log2(math.e)
VMEM = pl.BlockSpec(memory_space=pltpu.VMEM)
SMEM = pl.BlockSpec(memory_space=pltpu.SMEM)
HBM = pl.BlockSpec(memory_space=pltpu.HBM)


def attend_kernel(size, jobs, pieces, states, counts, holder_map, *refs):
    resumed, chained, left, ended = states
    refs = list(refs)

    def take(n):
        return [refs.pop(0) for _ in range(n)]

    (q_ref,) = take(1)
    new = take(size if any(job.fresh for job in jobs) else 0)
    far = dict(zip(pieces, take(len(pieces))))
    peak_in, sums_in = take(2) if resumed else (None, None)
    take(chained)
    peak_out, sums_out = take(2) if left else (None, None)
    o_ref, done, sem = take(3) if ended else (None, None, None)

    me, request = lax.axis_index("tensor"), lax.axis_index("request")
    holders = holder_map.shape[1]
    tokens = q_ref.shape[0]
    local_kv = new[0].shape[1] // (2 * HD) // size if new else max(job.head for job in jobs) + 1
    heads = q_ref.shape[1] // HD // (size * local_kv)
    rows = heads * tokens

    def bias_of(job):
        fresh = size * tokens if job.fresh else 0
        sizes = [(first, *far[first, job.distance].shape[:2]) for first in job.far]
        keys = fresh + sum(count * span for _, count, span in sizes)
        column = lax.broadcasted_iota(jnp.int32, (1, keys), 1)
        bias = jnp.zeros((1, keys), jnp.float32)
        if job.fresh:
            for d in range(1, size):
                hidden = jnp.bitwise_xor(me, d) > me
                here = (column >= tokens * d) & (column < tokens * (d + 1))
                bias = jnp.where(here & hidden, NEG, bias)
        start = fresh
        for first, count, span in sizes:
            for c in range(holders):
                place = lax.rem(request - holder_map[request, c] + holders, holders) - first
                at = start + place * span
                here = (column >= at) & (column < at + span)
                here &= (place >= 0) & (place < count) & (c >= counts[request])
                bias = jnp.where(here, NEG, bias)
            start += count * span
        return bias

    lead = -(-tokens // HD) * HD

    def with_causal(bias):
        row = lax.broadcasted_iota(jnp.int32, (tokens, lead), 0)
        col = lax.broadcasted_iota(jnp.int32, (tokens, lead), 1)
        return jnp.where((row < col) & (col < tokens), NEG, bias[:, :lead])

    def kind(job):
        return job.fresh, *((first, far[first, job.distance].shape[0]) for first in job.far)

    biases = {}
    for job in jobs:
        if kind(job) not in biases:
            bias = bias_of(job)
            biases[kind(job)] = bias, with_causal(bias) if job.fresh else None

    def side(job, which):
        blocks = []
        if job.fresh:
            head = jnp.bitwise_xor(me, job.distance) * local_kv + job.head
            at = pl.ds(pl.multiple_of((2 * head + which) * HD, HD), HD)
            blocks += [ref[:, at] for ref in new]
        at = slice((2 * job.head + which) * HD, (2 * job.head + which + 1) * HD)
        for first in job.far:
            piece = far[first, job.distance]
            blocks += [piece[s, :, at] for s in range(piece.shape[0])]
        return jnp.concatenate(blocks, axis=0)

    def columns(job, h=0, count=1):
        head = (jnp.bitwise_xor(me, job.distance) * local_kv + job.head) * heads + h
        return pl.ds(pl.multiple_of(head * HD, HD), count * HD)

    def scores_of(job):
        query = jnp.concatenate([q_ref[:, columns(job, h)] for h in range(heads)], axis=0)
        return lax.dot_general(
            query, side(job, 0), (((1,), (1,)), ((), ())), preferred_element_type=jnp.float32
        )

    copies = []

    def finish(job, scores):
        bias, causal = biases[kind(job)]
        keys = bias.shape[1]
        fit = [n for n in range(16, tokens + 1, 16) if tokens % n == 0 and n * keys <= CHUNK]
        chunk = max(fit, default=16)
        weights, scales = [], []
        for at in range(0, rows, chunk):
            here = slice(at, at + chunk)
            part = scores[here]
            if job.fresh:
                row = at % tokens
                part = jnp.concatenate(
                    [part[:, :lead] + causal[row : row + chunk], part[:, lead:] + bias[:, lead:]],
                    axis=1,
                )
            else:
                part = part + bias
            peak = jnp.broadcast_to(jnp.max(part, axis=1, keepdims=True), (chunk, HD))
            if job.resume is not None:
                before = peak_in[job.resume, here]
                peak = jnp.maximum(peak, before)
                scales.append(jnp.exp2((before - peak) * TO_EXP2))
            if job.leave is not None:
                peak_out[job.leave, here] = peak
            part = part - jnp.concatenate([peak] * (keys // HD), axis=1)
            weights.append(jnp.exp2(part * TO_EXP2).astype(jnp.bfloat16))
        value = side(job, 1)
        value = jnp.concatenate([value, jnp.ones_like(value)], axis=1)
        all_sums = jnp.dot(
            jnp.concatenate(weights, axis=0), value, preferred_element_type=jnp.float32
        )
        slot = len(copies)
        for n, at in enumerate(range(0, rows, chunk)):
            here = slice(at, at + chunk)
            sums = all_sums[here]
            if job.resume is not None:
                sums = sums + sums_in[job.resume, here] * jnp.concatenate([scales[n]] * 2, axis=1)
            if job.leave is not None:
                sums_out[job.leave, here] = sums
            else:
                h, row = at // tokens * HD, at % tokens
                out = (sums[:, :HD] / sums[:, HD:]).astype(o_ref.dtype)
                done[slot, row : row + chunk, h : h + HD] = out
        if job.leave is None:
            copy = pltpu.make_async_copy(
                done.at[slot], o_ref.at[:, columns(job, 0, heads)], sem.at[slot]
            )
            copy.start()
            copies.append(copy)

    scores = scores_of(jobs[0])
    for n, job in enumerate(jobs):
        later = scores_of(jobs[n + 1]) if n + 1 < len(jobs) else None
        finish(job, scores)
        scores = later
    for copy in copies:
        copy.wait()


class Job(typing.NamedTuple):
    distance: int
    head: int
    fresh: bool
    far: tuple
    resume: int | None
    leave: int | None


def attend(rules, query, new, far, jobs, state=None, out=None):
    pieces = tuple(far)
    tokens, columns = query.shape
    _, span, width = far[pieces[0]].shape if far else (0, 0, new[0].shape[1] // len(new))
    local_kv = width // (2 * HD)
    size = new[0].shape[1] // width
    heads = columns // HD // (size * local_kv)
    rows = heads * tokens
    left = sum(job.leave is not None for job in jobs)
    ended = len(jobs) - left
    fresh = any(job.fresh for job in jobs)
    operands = [query, *(new if fresh else ()), *far.values(), *(state or ())]
    chained = [out] if out is not None else []
    keys = [
        size * tokens * job.fresh + sum(far[first, job.distance].shape[0] * span for first in job.far)
        for job in jobs
    ]
    shapes, specs, scratch = [], [], []
    if left:
        shapes += [
            jax.ShapeDtypeStruct((left, rows, HD), jnp.float32),
            jax.ShapeDtypeStruct((left, rows, 2 * HD), jnp.float32),
        ]
        specs += [VMEM, VMEM]
    if ended:
        shapes += [jax.ShapeDtypeStruct(query.shape, query.dtype)]
        specs += [HBM]
        scratch = [
            pltpu.VMEM((ended, tokens, heads * HD), query.dtype),
            pltpu.SemaphoreType.DMA((ended,)),
        ]
    states = (state is not None, len(chained), left, ended)
    results = pl.pallas_call(
        functools.partial(attend_kernel, size, jobs, pieces, states),
        out_shape=shapes,
        in_specs=[SMEM, SMEM] + [VMEM] * len(operands) + [HBM] * len(chained),
        out_specs=specs,
        scratch_shapes=scratch,
        input_output_aliases={2 + len(operands): len(shapes) - 1} if chained else {},
        cost_estimate=pl.CostEstimate(
            flops=8 * HD * rows * sum(keys), bytes_accessed=0, transcendentals=rows * sum(keys)
        ),
        compiler_params=pltpu.CompilerParams(
            vmem_limit_bytes=16 * rows * max(keys) + 10 * 2**20
        ),
    )(*rules, *operands, *chained)
    return (results[:2] if left else None), (results[-1] if ended else None)


def local(size, holders, queries, kv_new, pool, counts, holder_map):
    query, new, pool = queries[0], kv_new[0], pool[0]
    request = lax.axis_index("request")
    rules = (counts, holder_map)
    half = size // 2
    inner = [half >> (n + 1) for n in range(half.bit_length() - 1)]

    def swap(piece, bit):
        return lax.ppermute(piece, "tensor", [(i, i ^ bit) for i in range(size)])

    def spread(piece, bits):
        held = {0: piece}
        for bit in bits:
            for distance in sorted(held):
                held[distance + bit] = swap(held[distance], bit)
        return [held[d] for d in sorted(held)]

    def after(piece, others):
        return lax.optimization_barrier((piece, others))[0]

    def span_of(r):
        return lax.dynamic_index_in_dim(pool, lax.rem(r, holders), 0, keepdims=True)

    new_away = swap(new, half)
    spans = [span_of(request)]
    for s in range(1, holders):
        pairs = [(i, (i + s) % holders) for i in range(holders)]
        spans.append(lax.ppermute(span_of(request + s), "request", pairs))
    early = jnp.concatenate(spans[:2], axis=0)
    early_away = swap(early, half)

    new = spread(new, inner) + spread(new_away, inner)
    local_kv = pool.shape[2] // (2 * HD)
    order = [(d, i) for d in range(size) for i in range(local_kv)]
    home, away = order[: len(order) // 2], order[len(order) // 2 :]

    late_away = swap(jnp.concatenate(spans[2:], axis=0), half)

    nearer, away = away[:1], away[1:]
    early_away = spread(early_away, inner)
    far = {(0, d): piece for d, piece in enumerate(spread(jnp.concatenate(spans, axis=0), inner))}
    far |= {(0, half + d): piece for d, piece in enumerate(early_away)}
    jobs = [Job(d, i, True, (0,), None, None) for d, i in home]
    jobs += [Job(d, i, True, (0,), None, n) for n, (d, i) in enumerate(away)]
    state, out = attend(rules, query, new, far, jobs)

    late_away = after(late_away, state)
    last = spread(late_away, inner)
    far = {(0, half): early_away[0], (2, half): late_away}
    jobs = [Job(d, i, True, (0, 2), None, None) for d, i in nearer]
    _, out = attend(rules, query, new, far, jobs, None, out)
    far = {(2, half + d): piece for d, piece in enumerate(last)}
    jobs = [Job(d, i, False, (2,), n, None) for n, (d, i) in enumerate(away)]
    return attend(rules, query, new, far, jobs, state, out)[1][None]


def solution(mesh):
    placed = (
        P(("group", "request"), "tensor", None),
        P(("group", "request"), "tensor", None),
        P(("group", "request"), None, None, "tensor"),
        P("group"),
        P("group", None),
    )
    return jax.shard_map(
        functools.partial(local, mesh.shape["tensor"], mesh.shape["request"]),
        mesh=mesh,
        in_specs=placed,
        out_specs=P(("group", "request"), "tensor", None),
        check_vma=False,
    )
```
